256 devices in a mesh: prow: 16 (over z_hi, y), pcol: 16 (over z_lo, x, core).
Axes of the slice: x: 4, y: 4, z: 8 (z_hi: 4, z_lo: 2; z = z_hi * 2 + z_lo), core: 2. Of those that a mesh axis runs over, the one named last changes fastest.
Arguments:
- sigma_ancestors: float32 [16384, 16384], P('prow', 'pcol'), as said below
- panel_two: float32 [16384, 256], P('pcol'), may hold values from -0.0546875 to 0.0546875
- panel_one: float32 [16384, 256], P('pcol'), may hold values from -0.0625 to 0.0625
- panel_top: float32 [256, 256], replicated, may hold values from -0.375 to 0.375
- blocks_two: int32 [48], replicated, may hold values from 0 to 63, as said below
- blocks_one: int32 [32], replicated, may hold values from 0 to 63, as said below
- inverse_two: float32 [256, 256], replicated, as said below
- inverse_one: float32 [256, 256], replicated, as said below
Outputs:
- column_two: float32 [16384, 256], P('prow')
- diagonal_two: float32 [256, 256], replicated
- column_one: float32 [16384, 256], P('prow')
- coupling_one: float32 [256, 256], replicated
- diagonal_one: float32 [256, 256], replicated
The draws below stay inside these ranges and needn't reach their ends.
Inputs may be any that keep to these rules, and one draw needn't show every extreme that they name: `blocks_two`: distinct and increasing; blocks 0, 32 and 63 are always listed. `blocks_one`: distinct and increasing, every one of them also listed in blocks_two; blocks 0, 32 and 63 are always listed. `sigma_ancestors`: symmetric positive definite. `inverse_two`: symmetric positive definite. `inverse_one`: symmetric positive definite.
All inputs are finite; a program needn't handle non-finite values.
Results may differ from the reference program's by a relative error of at most 0.000073.
Values sent between devices are 32-bit elements; how exact they have to be, the bound alone decides.
No kernel may reach another device: no remote copies, remote signals or barrier semaphores. Data moves between devices by JAX's collectives and lax.ppermute only.
A program may use at most 64 MiB of HBM per device.

```python
import math
import jax
import jax.numpy as jnp
from jax import lax

B = 256
NB = 64
K2 = 48
K1 = 32


def block_choice(key):
    order = jax.random.permutation(key, NB - 3).astype(jnp.int32) + 1
    middle = jnp.where(order < NB // 2, order, order + 1)
    return middle.astype(jnp.int32)


def fixed_blocks():
    return jnp.array([0, NB // 2, NB - 1], dtype=jnp.int32)


def draw_blocks_two(key, part):
    middle = block_choice(key)
    chosen = jnp.concatenate([fixed_blocks(), middle[:K2 - 3]])
    return jnp.sort(chosen).astype(jnp.int32)


def draw_blocks_one(key, part):
    middle = block_choice(key)
    chosen = jnp.concatenate([fixed_blocks(), middle[:K1 - 3]])
    return jnp.sort(chosen).astype(jnp.int32)


def symmetric_block(key, order, spread, coupling, diagonal):
    key_noise, key_scale = jax.random.split(key)
    noise = jax.random.normal(key_noise, (order, order), jnp.float32)
    scales = jnp.exp(jax.random.uniform(key_scale, (order,), jnp.float32, -spread, spread))
    mixed = (noise + noise.T) * (coupling / math.sqrt(order))
    count = jnp.arange(order, dtype=jnp.int32)
    identity = (count[:, None] == count[None, :]).astype(jnp.float32)
    return scales[:, None] * scales[None, :] * (diagonal * identity + mixed)


def draw_sigma_ancestors(key, part):
    key = jax.random.fold_in(key, 11)
    return symmetric_block(key, NB * B, 0.6, 0.7, 2.0)


def draw_inverse_two(key, part):
    key = jax.random.fold_in(key, 13)
    return symmetric_block(key, B, 0.4, 0.5, 1.5)


def draw_inverse_one(key, part):
    key = jax.random.fold_in(key, 17)
    return symmetric_block(key, B, 0.4, 0.5, 1.5)


def shard_levels(stream_key, extent, shards, smallest, high):
    loudness = 1.0
    for axis_at, shards_of in shards:
        heights = jax.random.uniform(jax.random.fold_in(jax.random.fold_in(stream_key, 6), axis_at), (shards_of,), jnp.float32, smallest / len(shards), high / len(shards))
        loudness = loudness * jnp.repeat(jnp.exp(heights), extent[axis_at] // shards_of).reshape((-1,) + (1,) * (len(extent) - 1 - axis_at))
    return loudness


def bell_draw(key, dims, deviation, bound, pieces=(), kind=jnp.bfloat16):
    result = jax.random.normal(key, dims, jnp.float32) * deviation
    if len(pieces) > 0:
        result = shard_levels(key, dims, pieces, -0.22, 0.18) * result
    return jnp.clip(result, min=-bound, max=bound).astype(kind)


def setup_inputs(seed: int = 0) -> dict:
    streams_of = jax.random.split(jax.random.key(seed), 9)
    sigma_ancestors = draw_sigma_ancestors(jax.random.fold_in(streams_of[8], 71), 0)
    panel_two = bell_draw(streams_of[1], (NB * B, B), (K2 * B) ** -0.5, 0.0546875, ((0, 16),), jnp.float32)
    panel_one = bell_draw(streams_of[2], (NB * B, B), (K1 * B) ** -0.5, 0.0625, ((0, 16),), jnp.float32)
    panel_top = bell_draw(streams_of[3], (B, B), B ** -0.5, 0.375, (), jnp.float32)
    blocks_two = draw_blocks_two(jax.random.fold_in(streams_of[8], 71), 0)
    blocks_one = draw_blocks_one(jax.random.fold_in(streams_of[8], 71), 0)
    inverse_two = draw_inverse_two(jax.random.fold_in(streams_of[8], 71), 0)
    inverse_one = draw_inverse_one(jax.random.fold_in(streams_of[8], 71), 0)
    return dict(sigma_ancestors=sigma_ancestors, panel_two=panel_two, panel_one=panel_one, panel_top=panel_top, blocks_two=blocks_two, blocks_one=blocks_one, inverse_two=inverse_two, inverse_one=inverse_one)


def product(left, right):
    return jnp.dot(left, right, precision=lax.Precision.HIGHEST, preferred_element_type=jnp.float32)


def inner(left, right):
    return lax.dot_general(left, right, (((0,), (0,)), ((), ())), precision=lax.Precision.HIGHEST, preferred_element_type=jnp.float32)


def block_mask(listed):
    block_ids = jnp.arange(NB, dtype=jnp.int32)
    flags = jnp.any(block_ids[:, None] == listed[None, :], axis=1).astype(jnp.float32)
    return jnp.repeat(flags, B)[:, None]


def reference(sigma_ancestors, panel_two, panel_one, panel_top, blocks_two, blocks_one, inverse_two, inverse_one):
    mask_two = block_mask(blocks_two)
    mask_one = block_mask(blocks_one)
    live_two = panel_two * mask_two
    live_one = panel_one * mask_one
    column_two = -mask_two * product(sigma_ancestors, live_two)
    diagonal_two = inverse_two - inner(live_two, column_two)
    coupling_one = -(product(diagonal_two, panel_top) + inner(column_two, live_one))
    column_one = -mask_one * (product(sigma_ancestors, live_one) + product(column_two, panel_top))
    diagonal_one = inverse_one - inner(live_one, column_one) - inner(panel_top, coupling_one)
    return column_two, diagonal_two, column_one, coupling_one, diagonal_one
```

```python
import functools

import jax
import jax.numpy as jnp
from jax import lax
from jax.experimental import pallas as pl
from jax.experimental.pallas import tpu as pltpu
from jax.sharding import Mesh, PartitionSpec as P

F32 = jnp.float32
BF16 = jnp.bfloat16
VMEM_LIMIT = 40 * 1024 * 1024
AXES = ("zh", "y", "zl", "x", "c")
SIZES = (4, 4, 2, 4, 2)
B = 256
CH = 64
ROWS = 1024


def split(value):
    high = value.astype(BF16)
    return high, (value - high.astype(F32)).astype(BF16)


def dot3(left, right, dims):
    lh, ll = left
    rh, rl = right
    go = functools.partial(lax.dot_general, dimension_numbers=(dims, ((), ())), preferred_element_type=F32)
    return go(lh, rh) + (go(lh, rl) + go(ll, rh))


MM = ((1,), (0,))
TM = ((0,), (0,))


def flag(listed, block):
    return jnp.max(jnp.where(listed == block, 1.0, 0.0), axis=1, keepdims=True)


def send_kernel(col_ref, s_ref, two_ref, one_ref, top_ref, b2_ref, b1_ref, p_ref, zh_ref, zl_ref):
    @pl.when(pl.program_id(0) == 0)
    def _():
        top = split(top_ref[...])
        first = col_ref[0] * (ROWS // B)
        for k in range(ROWS // B):
            rows = pl.ds(k * B, B)
            live_two = two_ref[rows, :] * flag(b2_ref[...], first + k)
            live_one = one_ref[rows, :] * flag(b1_ref[...], first + k)
            h2, l2 = split(live_two)
            hw, lw = split(live_one - dot3((h2, l2), top, MM))
            zh_ref[rows, :B] = h2
            zl_ref[rows, :B] = l2
            zh_ref[rows, B:] = hw
            zl_ref[rows, B:] = lw

    product_body(s_ref, zh_ref, zl_ref, p_ref)


def product_body(s_ref, zh_ref, zl_ref, p_ref):
    rows = s_ref.shape[0] * s_ref.shape[1]
    sigma = split(s_ref[...].reshape(rows, ROWS))
    p_ref[...] = dot3(sigma, (zh_ref[...], zl_ref[...]), MM)


def keep_kernel(col_ref, s_ref, zh_ref, zl_ref, p_ref):
    product_body(s_ref, zh_ref, zl_ref, p_ref)


def products(where, sigma, two, one, top, b2, b1):
    steps = 2
    per = 8 // steps
    sig = sigma.reshape(8, 2 * CH, ROWS)
    params = pltpu.CompilerParams(dimension_semantics=("arbitrary",), vmem_limit_bytes=VMEM_LIMIT)
    whole = lambda shape: pl.BlockSpec(shape, lambda i, w: (0,) * len(shape))
    out_p = pl.BlockSpec((per * CH, 2 * B), lambda i, w: (i, 0))
    send, zh, zl = pl.pallas_call(
        send_kernel,
        grid_spec=pltpu.PrefetchScalarGridSpec(
            num_scalar_prefetch=1,
            grid=(steps,),
            in_specs=[
                pl.BlockSpec((per, CH, ROWS), lambda i, w: (i, 1 - w[1], 0)),
                whole((ROWS, B)),
                whole((ROWS, B)),
                whole((B, B)),
                whole(b2.shape),
                whole(b1.shape),
            ],
            out_specs=[out_p, whole((ROWS, 2 * B)), whole((ROWS, 2 * B))],
        ),
        out_shape=[
            jax.ShapeDtypeStruct((8 * CH, 2 * B), F32),
            jax.ShapeDtypeStruct((ROWS, 2 * B), BF16),
            jax.ShapeDtypeStruct((ROWS, 2 * B), BF16),
        ],
        compiler_params=params,
        name="product_send",
    )(where, sig, two, one, top, b2, b1)

    got = lax.ppermute(send, "c", [(0, 1), (1, 0)])
    keep = pl.pallas_call(
        keep_kernel,
        grid_spec=pltpu.PrefetchScalarGridSpec(
            num_scalar_prefetch=1,
            grid=(steps,),
            in_specs=[
                pl.BlockSpec((per, CH, ROWS), lambda i, w: (i, w[1], 0)),
                whole((ROWS, 2 * B)),
                whole((ROWS, 2 * B)),
            ],
            out_specs=out_p,
        ),
        out_shape=jax.ShapeDtypeStruct((8 * CH, 2 * B), F32),
        compiler_params=params,
        cost_estimate=pl.CostEstimate(flops=3 * 2 * 512 * 1024 * 512, bytes_accessed=5 << 20, transcendentals=0),
        name="product_keep",
    )(where, sig, zh, zl)
    return keep + got


def gram_kernel(w_ref, y_ref, z_ref, top_ref, b2_ref, b1_ref, c2_ref, c1_ref, keep_ref, send_ref, g_ref):
    y = y_ref[pl.ds(0, CH), :]
    for k in range(1, 8):
        y = y + y_ref[pl.ds(k * CH, CH), :]
    block = w_ref[2]
    f2 = flag(b2_ref[...], block)
    f1 = flag(b1_ref[...], block)
    y2 = y[:, :B] * f2
    yw = y[:, B:]
    c2_ref[...] = -y2
    c1_ref[...] = -(yw * f1)
    live_two = split(z_ref[:, :B] * f2)
    w = split(z_ref[:, B:] * f1 - dot3(live_two, split(top_ref[...]), MM))
    yw = split(yw)
    g_ref[pl.ds(0, B), :] = dot3(live_two, split(y2), TM)
    g_ref[pl.ds(B, B), :] = dot3(live_two, yw, TM)
    g_ref[pl.ds(2 * B, B), :] = dot3(w, yw, TM)
    half = 3 * B // 2
    mine = w_ref[1]
    keep_ref[...] = g_ref[pl.ds(pl.multiple_of(mine * half, half), half), :]
    send_ref[...] = g_ref[pl.ds(pl.multiple_of((1 - mine) * half, half), half), :]


def gram(where, y, z, top, b2, b1):
    vm = pl.BlockSpec(memory_space=pltpu.VMEM)
    half = 3 * B // 2
    return pl.pallas_call(
        gram_kernel,
        in_specs=[pl.BlockSpec(memory_space=pltpu.SMEM)] + [vm] * 5,
        out_specs=[vm] * 4,
        out_shape=[
            jax.ShapeDtypeStruct((CH, B), F32),
            jax.ShapeDtypeStruct((CH, B), F32),
            jax.ShapeDtypeStruct((half, B), F32),
            jax.ShapeDtypeStruct((half, B), F32),
        ],
        scratch_shapes=[pltpu.VMEM((3 * B, B), F32)],
        compiler_params=pltpu.CompilerParams(vmem_limit_bytes=VMEM_LIMIT),
        name="gram",
    )(where, y, z, top, b2, b1)


def tops_kernel(top_ref, inv2_ref, inv1_ref, coup_ref, diag_ref):
    top = split(top_ref[...])
    it = dot3(split(inv2_ref[...]), top, MM)
    coup_ref[...] = it
    diag_ref[...] = inv1_ref[...] + dot3(top, split(it), TM)


def last_kernel(w_ref, mine_ref, other_ref, inv2_ref, it_ref, base_ref, d2_ref, cp_ref, d1_ref):
    half = 3 * B // 2

    def write(low, high):
        d2_ref[...] = inv2_ref[...] + low[pl.ds(0, B), :]
        cp_ref[pl.ds(0, B // 2), :] = low[pl.ds(B, B // 2), :] - it_ref[pl.ds(0, B // 2), :]
        cp_ref[pl.ds(B // 2, B // 2), :] = high[pl.ds(0, B // 2), :] - it_ref[pl.ds(B // 2, B // 2), :]
        d1_ref[...] = base_ref[...] + high[pl.ds(B // 2, B), :]

    @pl.when(w_ref[1] == 0)
    def _():
        write(mine_ref, other_ref)

    @pl.when(w_ref[1] == 1)
    def _():
        write(other_ref, mine_ref)


def a2a(value, axes):
    return lax.all_to_all(value, axes, 0, 0, tiled=True)


def per_device(sigma, two, one, top, blocks_two, blocks_one, inv2, inv1):
    zh, y, zl, x, c = (lax.axis_index(a) for a in AXES)
    row = zh * 4 + y
    col = zl * 8 + x * 2 + c
    where = jnp.stack([col, c, row * 4 + col // 4]).astype(jnp.int32)
    b2 = blocks_two.reshape(1, -1)
    b1 = blocks_one.reshape(1, -1)

    turn = [(i * 16 + j, j * 16 + i) for i in range(16) for j in range(16)]
    part = jnp.concatenate(
        [lax.dynamic_slice(p, (row * CH, 0), (CH, B)) for p in (two, one)], axis=1
    )
    z_rows = lax.ppermute(part, AXES, turn)

    pair = products(where, sigma, two, one, top, b2, b1)
    y_parts = a2a(pair, ("zl", "x"))
    c2, c1, keep, send = gram(where, y_parts, z_rows, top, b2, b1)
    column_two = lax.all_gather(c2, ("zl", "x", "c"), axis=0, tiled=True)
    column_one = lax.all_gather(c1, ("zl", "x", "c"), axis=0, tiled=True)

    vm = pl.BlockSpec(memory_space=pltpu.VMEM)
    square = jax.ShapeDtypeStruct((B, B), F32)
    it, base = pl.pallas_call(
        tops_kernel, in_specs=[vm] * 3, out_specs=[vm] * 2, out_shape=[square] * 2, name="tops"
    )(top, inv2, inv1)

    g = keep + lax.ppermute(send, "c", [(0, 1), (1, 0)])
    g = jnp.sum(a2a(g, ("y", "x")).reshape(16, 24, B), axis=0)
    g = jnp.broadcast_to(g[None], (8, 24, B)).reshape(8 * 24, B)
    g = jnp.sum(a2a(g, ("zh", "zl")).reshape(8, 24, B), axis=0)
    g = jnp.broadcast_to(g[None], (16, 24, B)).reshape(16 * 24, B)
    g = a2a(g, ("y", "x"))
    other = lax.ppermute(g, "c", [(0, 1), (1, 0)])
    d2, cp, d1 = pl.pallas_call(
        last_kernel,
        in_specs=[pl.BlockSpec(memory_space=pltpu.SMEM)] + [vm] * 5,
        out_specs=[vm] * 3,
        out_shape=[square] * 3,
        name="last",
    )(where, g, other, inv2, it, base)
    return column_two, d2, column_one, cp, d1


def solution(mesh):
    fine = Mesh(mesh.devices.reshape(SIZES), AXES)
    prow = ("zh", "y")
    pcol = ("zl", "x", "c")
    in_specs = (P(prow, pcol), P(pcol, None), P(pcol, None), P(), P(), P(), P(), P())
    out_specs = (P(prow, None), P(), P(prow, None), P(), P())
    return jax.shard_map(
        per_device, mesh=fine, in_specs=in_specs, out_specs=out_specs, check_vma=False
    )
```

```python
import functools

import jax
import jax.numpy as jnp
from jax import lax
from jax.experimental import pallas as pl
from jax.experimental.pallas import tpu as pltpu
from jax.sharding import Mesh, PartitionSpec as P

F32 = jnp.float32
BF16 = jnp.bfloat16
VMEM_LIMIT = 24 * 1024 * 1024
AXES = ("zh", "y", "zl", "x", "c")
SIZES = (4, 4, 2, 4, 2)
B = 256
W = 2 * B
CH = 64
CHIPS = 8
ROWS = 1024
HALF = 3 * B // 2
GR = HALF // CHIPS // 2
MM = ((1,), (0,))
TM = ((0,), (0,))
SWAP = [(0, 1), (1, 0)]
VM = pl.BlockSpec(memory_space=pltpu.VMEM)
SM = pl.BlockSpec(memory_space=pltpu.SMEM)
HBM = pl.BlockSpec(memory_space=pltpu.HBM)
LONG = pl.CostEstimate(flops=20 << 30, bytes_accessed=8 << 20, transcendentals=0)
TINY = pl.CostEstimate(flops=1, bytes_accessed=1, transcendentals=0)
PARAMS = pltpu.CompilerParams(vmem_limit_bytes=VMEM_LIMIT)


def split(value):
    high = value.astype(BF16)
    return high, (value - high.astype(F32)).astype(BF16)


def dot3(left, right, dims):
    lh, ll = left
    rh, rl = right
    go = functools.partial(lax.dot_general, dimension_numbers=(dims, ((), ())), preferred_element_type=F32)
    return go(lh, rh) + (go(lh, rl) + go(ll, rh))


def in_hbm(value):
    return pltpu.with_memory_space_constraint(value, pltpu.HBM)


def flag(listed, block):
    return jnp.max(jnp.where(listed == block, 1.0, 0.0), axis=1, keepdims=True)


def send_kernel(w_ref, s_hbm, two_hbm, one_hbm, top_hbm, b2_hbm, b1_hbm, p_ref, zh_ref, zl_ref,
                s_ref, two_ref, one_ref, top_ref, b2_ref, b1_ref, sems):
    steps = 2
    per = CHIPS // steps
    other = pl.multiple_of((1 - w_ref[1]) * CH, CH)
    pairs = [(b2_hbm, b2_ref), (b1_hbm, b1_ref), (top_hbm, top_ref), (two_hbm, two_ref), (one_hbm, one_ref)]
    for i in range(steps):
        pairs.append((s_hbm.at[pl.ds(i * per, per), pl.ds(other, CH), :], s_ref.at[pl.ds(i * per, per)]))
    copies = [pltpu.make_async_copy(src, dst, sems.at[i]) for i, (src, dst) in enumerate(pairs)]
    for copy in copies:
        copy.start()
    for copy in copies[:5]:
        copy.wait()
    top = split(top_ref[...])
    first = w_ref[0] * (ROWS // B)
    for k in range(ROWS // B):
        rows = pl.ds(k * B, B)
        live_two = two_ref[rows, :] * flag(b2_ref[...], first + k)
        live_one = one_ref[rows, :] * flag(b1_ref[...], first + k)
        h2, l2 = split(live_two)
        hw, lw = split(live_one - dot3((h2, l2), top, MM))
        zh_ref[rows, :B] = h2
        zl_ref[rows, :B] = l2
        zh_ref[rows, B:] = hw
        zl_ref[rows, B:] = lw
    z = (zh_ref[...], zl_ref[...])
    for i in range(steps):
        copies[5 + i].wait()
        sigma = split(s_ref[pl.ds(i * per, per)].reshape(per * CH, ROWS))
        p_ref[pl.ds(i * per * CH, per * CH), :] = dot3(sigma, z, MM)


def keep_kernel(w_ref, s_ref, zh_ref, zl_ref, p_ref):
    rows = s_ref.shape[0] * s_ref.shape[1]
    sigma = split(s_ref[...].reshape(rows, ROWS))
    p_ref[...] = dot3(sigma, (zh_ref[...], zl_ref[...]), MM)


def products(where, sigma, two, one, top, b2, b1, z_own):
    steps = 2
    per = CHIPS // steps
    sig = sigma.reshape(CHIPS, 2 * CH, ROWS)
    shape_p = jax.ShapeDtypeStruct((CHIPS * CH, W), F32)
    shape_z = jax.ShapeDtypeStruct((ROWS, W), BF16)
    send, zh, zl = pl.pallas_call(
        send_kernel,
        in_specs=[SM] + [HBM] * 6,
        out_specs=[VM] * 3,
        out_shape=[shape_p, shape_z, shape_z],
        scratch_shapes=[
            pltpu.VMEM((CHIPS, CH, ROWS), F32),
            pltpu.VMEM((ROWS, B), F32),
            pltpu.VMEM((ROWS, B), F32),
            pltpu.VMEM((B, B), F32),
            pltpu.VMEM(b2.shape, jnp.int32),
            pltpu.VMEM(b1.shape, jnp.int32),
            pltpu.SemaphoreType.DMA((7,)),
        ],
        compiler_params=PARAMS,
        cost_estimate=LONG,
        name="product_send",
    )(where, *map(in_hbm, (sig, two, one, top, b2, b1)))

    got = lax.ppermute(send, "c", SWAP)
    whole = lambda shape: pl.BlockSpec(shape, lambda i, w: (0,) * len(shape))
    keep = pl.pallas_call(
        keep_kernel,
        grid_spec=pltpu.PrefetchScalarGridSpec(
            num_scalar_prefetch=1,
            grid=(steps,),
            in_specs=[
                pl.BlockSpec((per, CH, ROWS), lambda i, w: (i, w[1], 0)),
                whole((ROWS, W)),
                whole((ROWS, W)),
            ],
            out_specs=pl.BlockSpec((per * CH, W), lambda i, w: (i, 0)),
        ),
        out_shape=shape_p,
        compiler_params=PARAMS,
        cost_estimate=LONG,
        name="product_keep",
    )(where, in_hbm(sig), zh, zl)
    keep, z_own = lax.optimization_barrier((keep, z_own))
    pair = pl.pallas_call(
        add_kernel, in_specs=[VM] * 2, out_specs=VM, out_shape=shape_p, compiler_params=PARAMS, name="pair_sum"
    )(keep, got)
    return pair, z_own


def add_kernel(left_ref, right_ref, out_ref):
    out_ref[...] = left_ref[...] + right_ref[...]


def chunk_kernel(w_ref, own_ref, b2_ref, b1_ref, top_ref, inv2_ref, inv1_ref, chunk_ref, it_ref, base_ref):
    block = w_ref[2]
    two = own_ref[:, :B] * -flag(b2_ref[...], block)
    one = own_ref[:, B:] * -flag(b1_ref[...], block)
    for q in range(CHIPS):
        chunk_ref[pl.ds(q * CH, CH), :B] = two
        chunk_ref[pl.ds(q * CH, CH), B:] = one
    top = split(top_ref[...])
    it = dot3(split(inv2_ref[...]), top, MM)
    it_ref[...] = it
    base_ref[...] = inv1_ref[...] + dot3(top, split(it), TM)


def spread_kernel(own_ref, across_ref, ahead_ref, behind_ref, out_ref):
    total = (own_ref[...] + across_ref[...]) + (ahead_ref[...] + behind_ref[...])
    for q in range(CHIPS):
        out_ref[pl.ds(q * GR, GR), :] = total


def gram_kernel(w_ref, y_own_ref, y_oth_ref, z_own_ref, z_oth_ref, top_ref, b2_ref, b1_ref, g_ref):
    block = w_ref[2]
    f2 = flag(b2_ref[...], block)
    f1 = flag(b1_ref[...], block)
    own = y_own_ref[...]
    z = jnp.concatenate([z_own_ref[...], z_oth_ref[...]], axis=0)
    live_two = z[:, :B] * f2

    def place(parts):
        rows = 0
        for part in parts:
            for low in range(0, part.shape[0], 8):
                q, rest = divmod(rows + low, 2 * GR)
                h, row = divmod(rest, GR)
                g_ref[pl.ds(q * GR + row, 8), pl.ds(h * B, B)] = part[low:low + 8]
            rows += part.shape[0]

    @pl.when(w_ref[1] == 0)
    def _():
        y = split(jnp.concatenate([own, y_oth_ref[...]], axis=0))
        place((
            dot3(split(live_two), [v[:, :B] for v in y], TM),
            dot3(split(live_two[:, :B // 2]), [v[:, B:] for v in y], TM),
        ))

    @pl.when(w_ref[1] == 1)
    def _():
        y = split(jnp.concatenate([own[:, B:], y_oth_ref[:, B:]], axis=0))
        live_w = z[:, B:] * f1 - dot3(split(live_two), split(top_ref[...]), MM)
        place((dot3(split(live_two[:, B // 2:]), y, TM), dot3(split(live_w), y, TM)))


def assemble_kernel(w_ref, own_ref, oth_ref, c2_ref, c1_ref):
    mine = w_ref[1]
    for core, ref in ((mine, own_ref), (1 - mine, oth_ref)):
        for q in range(CHIPS):
            rows = pl.ds(pl.multiple_of(q * 2 * CH + core * CH, CH), CH)
            c2_ref[rows, :] = ref[pl.ds(q * CH, CH), :B]
            c1_ref[rows, :] = ref[pl.ds(q * CH, CH), B:]


def last_kernel(w_ref, own_ref, oth_ref, inv2_ref, it_ref, base_ref, d2_ref, cp_ref, d1_ref):
    def write(refs):
        for half, ref in enumerate(refs):
            for q in range(CHIPS):
                for h in range(2):
                    at = half * HALF + q * 2 * GR + h * GR
                    piece = ref[pl.ds(q * GR, GR), pl.ds(h * B, B)]
                    for low in range(0, GR, 8):
                        which, row = divmod(at + low, B)
                        rows = pl.ds(row, 8)
                        value = piece[low:low + 8]
                        if which == 0:
                            d2_ref[rows, :] = inv2_ref[rows, :] + value
                        elif which == 1:
                            cp_ref[rows, :] = value - it_ref[rows, :]
                        else:
                            d1_ref[rows, :] = base_ref[rows, :] + value

    @pl.when(w_ref[1] == 0)
    def _():
        write((own_ref, oth_ref))

    @pl.when(w_ref[1] == 1)
    def _():
        write((oth_ref, own_ref))


def a2a(value, axes):
    return lax.all_to_all(value, axes, 0, 0, tiled=True)


def ring(value, axis):
    shift = lambda k: lax.ppermute(value, axis, [(i, (i + k) % 4) for i in range(4)])
    return value, shift(2), shift(1), shift(3)


def per_device(sigma, two, one, top, blocks_two, blocks_one, inv2, inv1):
    zh, y, zl, x, c = (lax.axis_index(a) for a in AXES)
    row = zh * 4 + y
    chip = zl * 4 + x
    where = jnp.stack([chip * 2 + c, c, row * 4 + lax.shift_right_logical(chip, 1)]).astype(jnp.int32)
    b2 = blocks_two.reshape(1, -1)
    b1 = blocks_one.reshape(1, -1)

    turn = [(i * 16 + j, j * 16 + i) for i in range(16) for j in range(16)]
    part = jnp.concatenate([lax.dynamic_slice(p, (row * CH, 0), (CH, B)) for p in (two, one)], axis=1)
    z_own = lax.ppermute(part, AXES, turn)

    pair, z_own = products(where, sigma, two, one, top, b2, b1, z_own)
    y_parts = a2a(pair, ("zl", "x"))
    z_oth = lax.ppermute(z_own, "c", SWAP)

    own = jnp.sum(y_parts.reshape(CHIPS, CH, W), axis=0)
    oth = lax.ppermute(own, "c", SWAP)
    parts = jax.ShapeDtypeStruct((CHIPS * GR, W), F32)
    g = pl.pallas_call(
        gram_kernel,
        in_specs=[SM] + [VM] * 7,
        out_specs=VM,
        out_shape=parts,
        compiler_params=PARAMS,
        name="gram",
    )(where, own, oth, z_own, z_oth, top, b2, b1)
    g, y_own = lax.optimization_barrier((g, own))
    g = a2a(g, ("zl", "x"))
    square = jax.ShapeDtypeStruct((B, B), F32)
    chunks, it, base = pl.pallas_call(
        chunk_kernel,
        in_specs=[SM] + [VM] * 6,
        out_specs=[VM] * 3,
        out_shape=[jax.ShapeDtypeStruct((CHIPS * CH, W), F32), square, square],
        compiler_params=PARAMS,
        name="chunks",
    )(where, y_own, b2, b1, top, inv2, inv1)
    chunks = a2a(chunks, ("zl", "x"))

    g = jnp.sum(g.reshape(CHIPS, GR, W), axis=0)
    own, across, ahead, behind = ring(g, "y")
    g = ring((own + across) + (ahead + behind), "zh")
    g = pl.pallas_call(
        spread_kernel, in_specs=[VM] * 4, out_specs=VM, out_shape=parts, compiler_params=PARAMS, name="spread"
    )(*g)
    g = a2a(g, ("zl", "x"))

    column = jax.ShapeDtypeStruct((ROWS, B), F32)
    column_two, column_one = pl.pallas_call(
        assemble_kernel,
        in_specs=[SM] + [VM] * 2,
        out_specs=[VM] * 2,
        out_shape=[column] * 2,
        compiler_params=PARAMS,
        name="assemble",
    )(where, chunks, lax.ppermute(chunks, "c", SWAP))
    g_oth = lax.ppermute(g, "c", SWAP)
    base, column_two, column_one = lax.optimization_barrier((base, column_two, column_one))
    d2, cp, d1 = pl.pallas_call(
        last_kernel,
        in_specs=[SM] + [VM] * 5,
        out_specs=[VM] * 3,
        out_shape=[square] * 3,
        compiler_params=PARAMS,
        name="last",
    )(where, g, g_oth, inv2, it, base)

    return column_two, d2, column_one, cp, d1


def solution(mesh):
    fine = Mesh(mesh.devices.reshape(SIZES), AXES)
    prow = ("zh", "y")
    pcol = ("zl", "x", "c")
    in_specs = (P(prow, pcol), P(pcol, None), P(pcol, None), P(), P(), P(), P(), P())
    out_specs = (P(prow, None), P(), P(prow, None), P(), P())
    return jax.shard_map(
        per_device, mesh=fine, in_specs=in_specs, out_specs=out_specs, check_vma=False
    )
```

```python
import functools

import jax
import jax.numpy as jnp
from jax import lax
from jax.experimental import pallas as pl
from jax.experimental.pallas import tpu as pltpu
from jax.sharding import Mesh, PartitionSpec as P

F32 = jnp.float32
BF16 = jnp.bfloat16
VMEM_LIMIT = 24 * 1024 * 1024
AXES = ("zh", "y", "zl", "x", "c")
SIZES = (4, 4, 2, 4, 2)
B = 256
W = 2 * B
CH = 64
CHIPS = 8
STEPS = 2
ROWS = 1024
HALF = 3 * B // 2
GR = HALF // CHIPS // 2
MM = ((1,), (0,))
TM = ((0,), (0,))
ROUTE = (
    0xCADEB16F, 0x52740983, 0xAEDC7695, 0x2F14803B, 0xBEF8C16D, 0x79A50432, 0x8EB91254, 0x3706FDAC,
    0x0218FDE7, 0x6453AC9B, 0x64315072, 0xDF8AEB9C, 0x29FB0341, 0xC567AED8, 0xC2513467, 0x08E9FDBA,
    0x43671025, 0xAE89CFDB, 0x46731052, 0x9AEFBC8D, 0x47561302, 0x98EDAFBC, 0x36407125, 0xCA9BFE8D,
    0x2430DEA1, 0xBC98F756, 0x421DBC8F, 0x5E9A3076, 0x0347E9AF, 0xD8CB5261, 0x6570F8DA, 0xB9CE2413,
)
SWAP = [(0, 1), (1, 0)]
VM = pl.BlockSpec(memory_space=pltpu.VMEM)
SM = pl.BlockSpec(memory_space=pltpu.SMEM)
HBM = pl.BlockSpec(memory_space=pltpu.HBM)
LONG = pl.CostEstimate(flops=20 << 30, bytes_accessed=8 << 20, transcendentals=0)
PARAMS = pltpu.CompilerParams(vmem_limit_bytes=VMEM_LIMIT)


def split(value):
    high = value.astype(BF16)
    return high, (value - high.astype(F32)).astype(BF16)


def dot3(left, right, dims):
    lh, ll = left
    rh, rl = right
    go = functools.partial(lax.dot_general, dimension_numbers=(dims, ((), ())), preferred_element_type=F32)
    return go(lh, rh) + (go(lh, rl) + go(ll, rh))


def in_hbm(value):
    return pltpu.with_memory_space_constraint(value, pltpu.HBM)


def flag(listed, block):
    return jnp.max(jnp.where(listed == block, 1.0, 0.0), axis=1, keepdims=True)


def product_rows(s_ref, low, high, z, p_ref):
    rows = split(s_ref[pl.ds(low, high - low)].reshape((high - low) * CH, ROWS))
    p_ref[pl.ds(low * CH, (high - low) * CH), :] = dot3(rows, z, MM)


def send_kernel(w_ref, s_hbm, two_hbm, one_hbm, top_hbm, b2_hbm, b1_hbm, p_ref, zh_ref, zl_ref, keep_ref,
                s_ref, two_ref, one_ref, top_ref, b2_ref, b1_ref, sems):
    per = CHIPS // STEPS
    blocks = ROWS // B

    def rows_of(core, i):
        return s_hbm.at[pl.ds(i * per, per), pl.ds(pl.multiple_of(core * CH, CH), CH), :]

    pairs = [(b2_hbm, b2_ref), (b1_hbm, b1_ref), (top_hbm, top_ref)]
    for k in range(blocks):
        rows = pl.ds(k * B, B)
        pairs += [(two_hbm.at[rows], two_ref.at[rows]), (one_hbm.at[rows], one_ref.at[rows])]
    for i in range(STEPS):
        pairs.append((rows_of(1 - w_ref[1], i), s_ref.at[pl.ds(i * per, per)]))
    for i in range(STEPS):
        pairs.append((rows_of(w_ref[1], i), keep_ref.at[pl.ds(i * per, per)]))
    copies = [pltpu.make_async_copy(src, dst, sems.at[i]) for i, (src, dst) in enumerate(pairs)]
    for copy in copies:
        copy.start()
    for copy in copies[:3]:
        copy.wait()
    top = split(top_ref[...])
    first = w_ref[0] * blocks
    for k in range(blocks):
        copies[3 + 2 * k].wait()
        copies[4 + 2 * k].wait()
        rows = pl.ds(k * B, B)
        live_two = two_ref[rows, :] * flag(b2_ref[...], first + k)
        live_one = one_ref[rows, :] * flag(b1_ref[...], first + k)
        h2, l2 = split(live_two)
        hw, lw = split(live_one - dot3((h2, l2), top, MM))
        zh_ref[rows, :B] = h2
        zl_ref[rows, :B] = l2
        zh_ref[rows, B:] = hw
        zl_ref[rows, B:] = lw
    z = (zh_ref[...], zl_ref[...])
    for i in range(STEPS):
        copies[3 + 2 * blocks + i].wait()
        product_rows(s_ref, i * per, (i + 1) * per, z, p_ref)
    for copy in copies[3 + 2 * blocks + STEPS:]:
        copy.wait()


def keep_kernel(s_ref, zh_ref, zl_ref, p_ref):
    z = (zh_ref[...], zl_ref[...])
    for i in range(STEPS):
        product_rows(s_ref, i * CHIPS // STEPS, (i + 1) * CHIPS // STEPS, z, p_ref)


def products(where, sigma, two, one, top, b2, b1, z_own):
    sigma = sigma.reshape(CHIPS, 2 * CH, ROWS)
    shape_p = jax.ShapeDtypeStruct((CHIPS * CH, W), F32)
    shape_z = jax.ShapeDtypeStruct((ROWS, W), BF16)
    shape_s = jax.ShapeDtypeStruct((CHIPS, CH, ROWS), F32)
    send, zh, zl, mine = pl.pallas_call(
        send_kernel,
        in_specs=[SM] + [HBM] * 6,
        out_specs=[VM] * 4,
        out_shape=[shape_p, shape_z, shape_z, shape_s],
        scratch_shapes=[
            pltpu.VMEM(shape_s.shape, F32),
            pltpu.VMEM((ROWS, B), F32),
            pltpu.VMEM((ROWS, B), F32),
            pltpu.VMEM((B, B), F32),
            pltpu.VMEM(b2.shape, jnp.int32),
            pltpu.VMEM(b1.shape, jnp.int32),
            pltpu.SemaphoreType.DMA((3 + 2 * (ROWS // B) + 2 * STEPS,)),
        ],
        compiler_params=PARAMS,
        cost_estimate=LONG,
        name="product_send",
    )(where, *map(in_hbm, (sigma, two, one, top, b2, b1)))

    got = lax.ppermute(send, "c", SWAP)
    keep = pl.pallas_call(
        keep_kernel,
        in_specs=[VM] * 3,
        out_specs=VM,
        out_shape=shape_p,
        compiler_params=PARAMS,
        cost_estimate=LONG,
        name="product_keep",
    )(mine, zh, zl)
    keep, z_own = lax.optimization_barrier((keep, z_own))
    pair = pl.pallas_call(
        add_kernel, in_specs=[VM] * 2, out_specs=VM, out_shape=shape_p, compiler_params=PARAMS, name="pair_sum"
    )(keep, got)
    return pair, z_own


def add_kernel(left_ref, right_ref, out_ref):
    out_ref[...] = left_ref[...] + right_ref[...]


def chunk_kernel(w_ref, own_ref, b2_ref, b1_ref, top_ref, inv2_ref, inv1_ref, chunk_ref, it_ref, base_ref):
    block = w_ref[2]
    two = own_ref[:, :B] * -flag(b2_ref[...], block)
    one = own_ref[:, B:] * -flag(b1_ref[...], block)
    for q in range(CHIPS):
        chunk_ref[pl.ds(q * CH, CH), :B] = two
        chunk_ref[pl.ds(q * CH, CH), B:] = one
    top = split(top_ref[...])
    it = dot3(split(inv2_ref[...]), top, MM)
    it_ref[...] = it
    base_ref[...] = inv1_ref[...] + dot3(top, split(it), TM)


def spread_kernel(own_ref, across_ref, ahead_ref, behind_ref, out_ref):
    total = (own_ref[...] + across_ref[...]) + (ahead_ref[...] + behind_ref[...])
    for q in range(CHIPS):
        out_ref[pl.ds(q * GR, GR), :] = total


def gram_kernel(w_ref, y_own_ref, y_oth_ref, z_own_ref, z_oth_ref, top_ref, b2_ref, b1_ref, g_ref):
    block = w_ref[2]
    f2 = flag(b2_ref[...], block)
    f1 = flag(b1_ref[...], block)
    own = y_own_ref[...]
    z = jnp.concatenate([z_own_ref[...], z_oth_ref[...]], axis=0)
    live_two = z[:, :B] * f2

    def place(parts):
        rows = 0
        for part in parts:
            for low in range(0, part.shape[0], 8):
                q, rest = divmod(rows + low, 2 * GR)
                h, row = divmod(rest, GR)
                g_ref[pl.ds(q * GR + row, 8), pl.ds(h * B, B)] = part[low:low + 8]
            rows += part.shape[0]

    @pl.when(w_ref[1] == 0)
    def _():
        y = split(jnp.concatenate([own, y_oth_ref[...]], axis=0))
        place((
            dot3(split(live_two), [v[:, :B] for v in y], TM),
            dot3(split(live_two[:, :B // 2]), [v[:, B:] for v in y], TM),
        ))

    @pl.when(w_ref[1] == 1)
    def _():
        y = split(jnp.concatenate([own[:, B:], y_oth_ref[:, B:]], axis=0))
        live_w = z[:, B:] * f1 - dot3(split(live_two), split(top_ref[...]), MM)
        place((dot3(split(live_two[:, B // 2:]), y, TM), dot3(split(live_w), y, TM)))


def assemble_kernel(w_ref, own_ref, oth_ref, c2_ref, c1_ref):
    mine = w_ref[1]
    for core, ref in ((mine, own_ref), (1 - mine, oth_ref)):
        for q in range(CHIPS):
            rows = pl.ds(pl.multiple_of(q * 2 * CH + core * CH, CH), CH)
            c2_ref[rows, :] = ref[pl.ds(q * CH, CH), :B]
            c1_ref[rows, :] = ref[pl.ds(q * CH, CH), B:]


def last_kernel(w_ref, own_ref, oth_ref, inv2_ref, it_ref, base_ref, d2_ref, cp_ref, d1_ref):
    def write(refs):
        for half, ref in enumerate(refs):
            for q in range(CHIPS):
                for h in range(2):
                    at = half * HALF + q * 2 * GR + h * GR
                    piece = ref[pl.ds(q * GR, GR), pl.ds(h * B, B)]
                    for low in range(0, GR, 8):
                        which, row = divmod(at + low, B)
                        rows = pl.ds(row, 8)
                        value = piece[low:low + 8]
                        if which == 0:
                            d2_ref[rows, :] = inv2_ref[rows, :] + value
                        elif which == 1:
                            cp_ref[rows, :] = value - it_ref[rows, :]
                        else:
                            d1_ref[rows, :] = base_ref[rows, :] + value

    @pl.when(w_ref[1] == 0)
    def _():
        write((own_ref, oth_ref))

    @pl.when(w_ref[1] == 1)
    def _():
        write((oth_ref, own_ref))


def route(i, j):
    return (ROUTE[2 * j + (i >> 3)] >> (4 * (i & 7))) & 15


def a2a(value, axes):
    return lax.all_to_all(value, axes, 0, 0, tiled=True)


def ring(value, axis):
    shift = lambda k: lax.ppermute(value, axis, [(i, (i + k) % 4) for i in range(4)])
    return value, shift(2), shift(1), shift(3)


def per_device(sigma, two, one, top, blocks_two, blocks_one, inv2, inv1):
    zh, y, zl, x, c = (lax.axis_index(a) for a in AXES)
    row = zh * 4 + y
    chip = zl * 4 + x
    where = jnp.stack([chip * 2 + c, c, row * 4 + lax.shift_right_logical(chip, 1)]).astype(jnp.int32)
    b2 = blocks_two.reshape(1, -1)
    b1 = blocks_one.reshape(1, -1)

    turn = [(i * 16 + j, j * 16 + route(i, j)) for i in range(16) for j in range(16)]
    word = jnp.uint32(ROUTE[0])
    for k, other in enumerate(ROUTE):
        word = jnp.where((chip * 2 + c) * 2 + lax.shift_right_logical(row, 3) == k, jnp.uint32(other), word)
    chunk = (lax.shift_right_logical(word, (4 * (row & 7)).astype(jnp.uint32)) & 15).astype(jnp.int32)
    part = jnp.concatenate([lax.dynamic_slice(p, (chunk * CH, 0), (CH, B)) for p in (two, one)], axis=1)
    z_own = lax.ppermute(part, AXES, turn)

    pair, z_own = products(where, sigma, two, one, top, b2, b1, z_own)
    y_parts = a2a(pair, ("zl", "x"))
    z_oth = lax.ppermute(z_own, "c", SWAP)

    own = jnp.sum(y_parts.reshape(CHIPS, CH, W), axis=0)
    oth = lax.ppermute(own, "c", SWAP)
    parts = jax.ShapeDtypeStruct((CHIPS * GR, W), F32)
    g = pl.pallas_call(
        gram_kernel,
        in_specs=[SM] + [VM] * 7,
        out_specs=VM,
        out_shape=parts,
        compiler_params=PARAMS,
        name="gram",
    )(where, own, oth, z_own, z_oth, top, b2, b1)
    g, y_own = lax.optimization_barrier((g, own))
    g = a2a(g, ("zl", "x"))
    square = jax.ShapeDtypeStruct((B, B), F32)
    chunks, it, base = pl.pallas_call(
        chunk_kernel,
        in_specs=[SM] + [VM] * 6,
        out_specs=[VM] * 3,
        out_shape=[jax.ShapeDtypeStruct((CHIPS * CH, W), F32), square, square],
        compiler_params=PARAMS,
        name="chunks",
    )(where, y_own, b2, b1, top, inv2, inv1)
    chunks = a2a(chunks, ("zl", "x"))

    g = jnp.sum(g.reshape(CHIPS, GR, W), axis=0)
    own, across, ahead, behind = ring(g, "y")
    g = ring((own + across) + (ahead + behind), "zh")
    g = pl.pallas_call(
        spread_kernel, in_specs=[VM] * 4, out_specs=VM, out_shape=parts, compiler_params=PARAMS, name="spread"
    )(*g)
    g = a2a(g, ("zl", "x"))

    column = jax.ShapeDtypeStruct((ROWS, B), F32)
    column_two, column_one = pl.pallas_call(
        assemble_kernel,
        in_specs=[SM] + [VM] * 2,
        out_specs=[VM] * 2,
        out_shape=[column] * 2,
        compiler_params=PARAMS,
        name="assemble",
    )(where, chunks, lax.ppermute(chunks, "c", SWAP))
    g_oth = lax.ppermute(g, "c", SWAP)
    base, column_two, column_one = lax.optimization_barrier((base, column_two, column_one))
    d2, cp, d1 = pl.pallas_call(
        last_kernel,
        in_specs=[SM] + [VM] * 5,
        out_specs=[VM] * 3,
        out_shape=[square] * 3,
        compiler_params=PARAMS,
        name="last",
    )(where, g, g_oth, inv2, it, base)

    return column_two, d2, column_one, cp, d1


def solution(mesh):
    fine = Mesh(mesh.devices.reshape(SIZES), AXES)
    prow = ("zh", "y")
    pcol = ("zl", "x", "c")
    in_specs = (P(prow, pcol), P(pcol, None), P(pcol, None), P(), P(), P(), P(), P())
    out_specs = (P(prow, None), P(), P(prow, None), P(), P())
    return jax.shard_map(
        per_device, mesh=fine, in_specs=in_specs, out_specs=out_specs, check_vma=False
    )
```

```python
import functools

import jax
import jax.numpy as jnp
from jax import lax
from jax.experimental import pallas as pl
from jax.experimental.pallas import tpu as pltpu
from jax.sharding import Mesh, PartitionSpec as P

F32 = jnp.float32
BF16 = jnp.bfloat16
VMEM_LIMIT = 24 * 1024 * 1024
AXES = ("zh", "y", "zl", "x", "c")
SIZES = (4, 4, 2, 4, 2)
B = 256
W = 2 * B
CH = 64
CHIPS = 8
STEPS = 2
ROWS = 1024
HALF = 3 * B // 2
GR = HALF // CHIPS // 2
MM = ((1,), (0,))
TM = ((0,), (0,))
ROUTE = (
    0xCADEB16F, 0x52740983, 0xAEDC7695, 0x2F14803B, 0xBEF8C16D, 0x79A50432, 0x8EB91254, 0x3706FDAC,
    0x0218FDE7, 0x6453AC9B, 0x64315072, 0xDF8AEB9C, 0x29FB0341, 0xC567AED8, 0xC2513467, 0x08E9FDBA,
    0x43671025, 0xAE89CFDB, 0x46731052, 0x9AEFBC8D, 0x47561302, 0x98EDAFBC, 0x36407125, 0xCA9BFE8D,
    0x2430DEA1, 0xBC98F756, 0x421DBC8F, 0x5E9A3076, 0x0347E9AF, 0xD8CB5261, 0x6570F8DA, 0xB9CE2413,
)
SWAP = [(0, 1), (1, 0)]
VM = pl.BlockSpec(memory_space=pltpu.VMEM)
SM = pl.BlockSpec(memory_space=pltpu.SMEM)
HBM = pl.BlockSpec(memory_space=pltpu.HBM)
LONG = pl.CostEstimate(flops=20 << 30, bytes_accessed=8 << 20, transcendentals=0)
LONGER = pl.CostEstimate(flops=20 << 30, bytes_accessed=8 << 20, transcendentals=0)
PARAMS = pltpu.CompilerParams(vmem_limit_bytes=VMEM_LIMIT)


def split(value):
    high = value.astype(BF16)
    return high, (value - high.astype(F32)).astype(BF16)


def dot3(left, right, dims):
    lh, ll = left
    rh, rl = right
    go = functools.partial(lax.dot_general, dimension_numbers=(dims, ((), ())), preferred_element_type=F32)
    return go(lh, rh) + (go(lh, rl) + go(ll, rh))


def in_hbm(value):
    return pltpu.with_memory_space_constraint(value, pltpu.HBM)


def flag(listed, block):
    return jnp.max(jnp.where(listed == block, 1.0, 0.0), axis=1, keepdims=True)


def product_rows(s_ref, low, high, z, p_ref):
    rows = split(s_ref[pl.ds(low, high - low)].reshape((high - low) * CH, ROWS))
    p_ref[pl.ds(low * CH, (high - low) * CH), :] = dot3(rows, z, MM)


def send_kernel(w_ref, s_hbm, two_hbm, one_hbm, top_hbm, b2_hbm, b1_hbm, p_ref, zh_ref, zl_ref, keep_ref, part_ref,
                s_ref, two_ref, one_ref, top_ref, b2_ref, b1_ref, sems):
    per = CHIPS // STEPS
    blocks = ROWS // B

    def rows_of(core, i):
        return s_hbm.at[pl.ds(i * per, per), pl.ds(pl.multiple_of(core * CH, CH), CH), :]

    pairs = [(b2_hbm, b2_ref), (b1_hbm, b1_ref), (top_hbm, top_ref)]
    for k in range(blocks):
        rows = pl.ds(k * B, B)
        pairs += [(two_hbm.at[rows], two_ref.at[rows]), (one_hbm.at[rows], one_ref.at[rows])]
    for i in range(STEPS):
        pairs.append((rows_of(1 - w_ref[1], i), s_ref.at[pl.ds(i * per, per)]))
    for i in range(STEPS):
        pairs.append((rows_of(w_ref[1], i), keep_ref.at[pl.ds(i * per, per)]))
    copies = [pltpu.make_async_copy(src, dst, sems.at[i]) for i, (src, dst) in enumerate(pairs)]
    for copy in copies:
        copy.start()
    for copy in copies[:3]:
        copy.wait()
    top = split(top_ref[...])
    first = w_ref[0] * blocks
    for k in range(blocks):
        copies[3 + 2 * k].wait()
        copies[4 + 2 * k].wait()
        rows = pl.ds(k * B, B)
        live_two = two_ref[rows, :] * flag(b2_ref[...], first + k)
        live_one = one_ref[rows, :] * flag(b1_ref[...], first + k)
        h2, l2 = split(live_two)
        hw, lw = split(live_one - dot3((h2, l2), top, MM))
        zh_ref[rows, :B] = h2
        zl_ref[rows, :B] = l2
        zh_ref[rows, B:] = hw
        zl_ref[rows, B:] = lw
    chunk = pl.ds(pl.multiple_of(w_ref[3] * CH, CH), CH)
    part_ref[:, :B] = two_ref[chunk, :]
    part_ref[:, B:] = one_ref[chunk, :]
    z = (zh_ref[...], zl_ref[...])
    for i in range(STEPS):
        copies[3 + 2 * blocks + i].wait()
        product_rows(s_ref, i * per, (i + 1) * per, z, p_ref)
    for copy in copies[3 + 2 * blocks + STEPS:]:
        copy.wait()


def keep_kernel(s_ref, zh_ref, zl_ref, p_ref):
    z = (zh_ref[...], zl_ref[...])
    for i in range(STEPS):
        product_rows(s_ref, i * CHIPS // STEPS, (i + 1) * CHIPS // STEPS, z, p_ref)


def products(where, sigma, two, one, top, b2, b1):
    sigma = sigma.reshape(CHIPS, 2 * CH, ROWS)
    shape_p = jax.ShapeDtypeStruct((CHIPS * CH, W), F32)
    shape_z = jax.ShapeDtypeStruct((ROWS, W), BF16)
    shape_s = jax.ShapeDtypeStruct((CHIPS, CH, ROWS), F32)
    send, zh, zl, mine, part = pl.pallas_call(
        send_kernel,
        in_specs=[SM] + [HBM] * 6,
        out_specs=[VM] * 5,
        out_shape=[shape_p, shape_z, shape_z, shape_s, jax.ShapeDtypeStruct((CH, W), F32)],
        scratch_shapes=[
            pltpu.VMEM(shape_s.shape, F32),
            pltpu.VMEM((ROWS, B), F32),
            pltpu.VMEM((ROWS, B), F32),
            pltpu.VMEM((B, B), F32),
            pltpu.VMEM(b2.shape, jnp.int32),
            pltpu.VMEM(b1.shape, jnp.int32),
            pltpu.SemaphoreType.DMA((3 + 2 * (ROWS // B) + 2 * STEPS,)),
        ],
        compiler_params=PARAMS,
        cost_estimate=LONG,
        name="product_send",
    )(where, *map(in_hbm, (sigma, two, one, top, b2, b1)))

    got = lax.ppermute(send, "c", SWAP)
    keep = pl.pallas_call(
        keep_kernel,
        in_specs=[VM] * 3,
        out_specs=VM,
        out_shape=shape_p,
        compiler_params=PARAMS,
        cost_estimate=LONG,
        name="product_keep",
    )(mine, zh, zl)
    pair = pl.pallas_call(
        add_kernel, in_specs=[VM] * 2, out_specs=VM, out_shape=shape_p, compiler_params=PARAMS, name="pair_sum"
    )(keep, got)
    return pair, part


def sum_kernel(parts, in_ref, after_ref, out_ref):
    rows = out_ref.shape[0]
    total = in_ref[pl.ds(0, rows), :]
    for k in range(1, parts):
        total = total + in_ref[pl.ds(k * rows, rows), :]
    out_ref[...] = total


def sum_parts(value, after):
    rows = value.shape[0] // CHIPS
    return pl.pallas_call(
        functools.partial(sum_kernel, CHIPS),
        in_specs=[VM, pl.BlockSpec(memory_space=pl.ANY)],
        out_specs=VM,
        out_shape=jax.ShapeDtypeStruct((rows, W), F32),
        compiler_params=PARAMS,
        name="sum_parts",
    )(value, after)


def ring_kernel(own_ref, behind_ref, ahead_ref, across_ref, out_ref):
    out_ref[...] = (own_ref[...] + across_ref[...]) + (ahead_ref[...] + behind_ref[...])


def add_kernel(left_ref, right_ref, out_ref):
    out_ref[...] = left_ref[...] + right_ref[...]


def chunk_kernel(w_ref, own_ref, b2_ref, b1_ref, top_ref, inv2_ref, inv1_ref, chunk_ref, it_ref, base_ref):
    block = w_ref[2]
    two = own_ref[:, :B] * -flag(b2_ref[...], block)
    one = own_ref[:, B:] * -flag(b1_ref[...], block)
    for q in range(CHIPS):
        chunk_ref[pl.ds(q * CH, CH), :B] = two
        chunk_ref[pl.ds(q * CH, CH), B:] = one
    top = split(top_ref[...])
    it = dot3(split(inv2_ref[...]), top, MM)
    it_ref[...] = it
    base_ref[...] = inv1_ref[...] + dot3(top, split(it), TM)


def spread_kernel(own_ref, behind_ref, ahead_ref, across_ref, out_ref):
    total = (own_ref[...] + across_ref[...]) + (ahead_ref[...] + behind_ref[...])
    for q in range(CHIPS):
        out_ref[pl.ds(q * GR, GR), :] = total


def rows_kernel(w_ref, z_ref, top_ref, b2_ref, b1_ref, live_ref):
    block = w_ref[2]
    live_two = z_ref[:, :B] * flag(b2_ref[...], block)
    live_one = z_ref[:, B:] * flag(b1_ref[...], block)
    live_ref[:, :B] = live_two
    live_ref[:, B:] = live_one - dot3(split(live_two), split(top_ref[...]), MM)


def gram_kernel(w_ref, own_ref, oth_ref, z_own_ref, z_oth_ref, g_ref):
    def place(parts):
        rows = 0
        for part in parts:
            for low in range(0, part.shape[0], 8):
                q, rest = divmod(rows + low, 2 * GR)
                h, row = divmod(rest, GR)
                g_ref[pl.ds(q * GR + row, 8), pl.ds(h * B, B)] = part[low:low + 8]
            rows += part.shape[0]

    z = split(jnp.concatenate([z_own_ref[...], z_oth_ref[...]], axis=0))

    def columns(pair, low, high):
        return [v[:, low:high] for v in pair]

    @pl.when(w_ref[1] == 0)
    def _():
        y = split(jnp.concatenate([own_ref[...], oth_ref[...]], axis=0))
        place((
            dot3(columns(z, 0, B), columns(y, 0, B), TM),
            dot3(columns(z, 0, B // 2), columns(y, B, W), TM),
        ))

    @pl.when(w_ref[1] == 1)
    def _():
        y = split(jnp.concatenate([own_ref[:, B:], oth_ref[:, B:]], axis=0))
        place((dot3(columns(z, B // 2, B), y, TM), dot3(columns(z, B, W), y, TM)))


def assemble_kernel(w_ref, own_ref, oth_ref, c2_ref, c1_ref):
    mine = w_ref[1]
    for core, ref in ((mine, own_ref), (1 - mine, oth_ref)):
        for q in range(CHIPS):
            rows = pl.ds(pl.multiple_of(q * 2 * CH + core * CH, CH), CH)
            c2_ref[rows, :] = ref[pl.ds(q * CH, CH), :B]
            c1_ref[rows, :] = ref[pl.ds(q * CH, CH), B:]


def last_kernel(w_ref, own_ref, oth_ref, inv2_ref, it_ref, base_ref, d2_ref, cp_ref, d1_ref):
    def write(refs):
        for half, ref in enumerate(refs):
            for q in range(CHIPS):
                for h in range(2):
                    at = half * HALF + q * 2 * GR + h * GR
                    piece = ref[pl.ds(q * GR, GR), pl.ds(h * B, B)]
                    for low in range(0, GR, 8):
                        which, row = divmod(at + low, B)
                        rows = pl.ds(row, 8)
                        value = piece[low:low + 8]
                        if which == 0:
                            d2_ref[rows, :] = inv2_ref[rows, :] + value
                        elif which == 1:
                            cp_ref[rows, :] = value - it_ref[rows, :]
                        else:
                            d1_ref[rows, :] = base_ref[rows, :] + value

    @pl.when(w_ref[1] == 0)
    def _():
        write((own_ref, oth_ref))

    @pl.when(w_ref[1] == 1)
    def _():
        write((oth_ref, own_ref))


def route(i, j):
    return (ROUTE[2 * j + (i >> 3)] >> (4 * (i & 7))) & 15


def a2a(value, axes):
    return lax.all_to_all(value, axes, 0, 0, tiled=True)


def ring(value, axis):
    shift = lambda k: lax.ppermute(value, axis, [(i, (i + k) % 4) for i in range(4)])
    return value, shift(3), shift(1), shift(2)


def per_device(sigma, two, one, top, blocks_two, blocks_one, inv2, inv1):
    z_hi, y, z_lo, x, c = (lax.axis_index(a) for a in AXES)
    row = z_hi * 4 + y
    chip = z_lo * 4 + x
    b2 = blocks_two.reshape(1, -1)
    b1 = blocks_one.reshape(1, -1)

    turn = [(i * 16 + j, j * 16 + route(i, j)) for i in range(16) for j in range(16)]
    word = jnp.uint32(ROUTE[0])
    for k, other in enumerate(ROUTE):
        word = jnp.where((chip * 2 + c) * 2 + lax.shift_right_logical(row, 3) == k, jnp.uint32(other), word)
    chunk = (lax.shift_right_logical(word, (4 * (row & 7)).astype(jnp.uint32)) & 15).astype(jnp.int32)
    where = jnp.stack([chip * 2 + c, c, row * 4 + lax.shift_right_logical(chip, 1), chunk]).astype(jnp.int32)
    pair, part = products(where, sigma, two, one, top, b2, b1)
    z_own = lax.ppermute(part, AXES, turn)
    y_parts = a2a(pair, ("zl", "x"))
    z_own = pl.pallas_call(
        rows_kernel,
        in_specs=[SM] + [VM] * 4,
        out_specs=VM,
        out_shape=jax.ShapeDtypeStruct((CH, W), F32),
        compiler_params=PARAMS,
        cost_estimate=LONGER,
        name="panel_rows",
    )(where, z_own, top, b2, b1)
    z_oth = lax.ppermute(z_own, "c", SWAP)
    own = sum_parts(y_parts, z_own)
    oth = lax.ppermute(own, "c", SWAP)
    parts = jax.ShapeDtypeStruct((CHIPS * GR, W), F32)
    g = pl.pallas_call(
        gram_kernel,
        in_specs=[SM] + [VM] * 4,
        out_specs=VM,
        out_shape=parts,
        compiler_params=PARAMS,
        name="gram",
    )(where, own, oth, z_own, z_oth)
    g, y_own = lax.optimization_barrier((g, own))
    g = a2a(g, ("zl", "x"))
    square = jax.ShapeDtypeStruct((B, B), F32)
    chunks, it, base = pl.pallas_call(
        chunk_kernel,
        in_specs=[SM] + [VM] * 6,
        out_specs=[VM] * 3,
        out_shape=[jax.ShapeDtypeStruct((CHIPS * CH, W), F32), square, square],
        compiler_params=PARAMS,
        name="chunks",
    )(where, y_own, b2, b1, top, inv2, inv1)
    chunks = a2a(chunks, ("zl", "x"))

    g = sum_parts(g, base)
    g = pl.pallas_call(
        ring_kernel, in_specs=[VM] * 4, out_specs=VM, out_shape=jax.ShapeDtypeStruct((GR, W), F32),
        compiler_params=PARAMS, name="ring_sum",
    )(*ring(g, "y"))
    g = ring(g, "zh")
    g = pl.pallas_call(
        spread_kernel, in_specs=[VM] * 4, out_specs=VM, out_shape=parts, compiler_params=PARAMS, name="spread"
    )(*g)
    g = a2a(g, ("zl", "x"))

    column = jax.ShapeDtypeStruct((ROWS, B), F32)
    column_two, column_one = pl.pallas_call(
        assemble_kernel,
        in_specs=[SM] + [VM] * 2,
        out_specs=[VM] * 2,
        out_shape=[column] * 2,
        compiler_params=PARAMS,
        name="assemble",
    )(where, chunks, lax.ppermute(chunks, "c", SWAP))
    g_oth = lax.ppermute(g, "c", SWAP)
    base, column_two, column_one = lax.optimization_barrier((base, column_two, column_one))
    d2, cp, d1 = pl.pallas_call(
        last_kernel,
        in_specs=[SM] + [VM] * 5,
        out_specs=[VM] * 3,
        out_shape=[square] * 3,
        compiler_params=PARAMS,
        name="last",
    )(where, g, g_oth, inv2, it, base)

    return column_two, d2, column_one, cp, d1


def solution(mesh):
    fine = Mesh(mesh.devices.reshape(SIZES), AXES)
    prow = ("zh", "y")
    pcol = ("zl", "x", "c")
    in_specs = (P(prow, pcol), P(pcol, None), P(pcol, None), P(), P(), P(), P(), P())
    out_specs = (P(prow, None), P(), P(prow, None), P(), P())
    return jax.shard_map(
        per_device, mesh=fine, in_specs=in_specs, out_specs=out_specs, check_vma=False
    )
```

```python
import functools

import jax
import jax.numpy as jnp
from jax import lax
from jax.experimental import pallas as pl
from jax.experimental.pallas import tpu as pltpu
from jax.sharding import Mesh, PartitionSpec as P

F32 = jnp.float32
BF16 = jnp.bfloat16
VMEM_LIMIT = 24 * 1024 * 1024
AXES = ("zh", "y", "zl", "x", "c")
SIZES = (4, 4, 2, 4, 2)
B = 256
W = 2 * B
CH = 64
CHIPS = 8
STEPS = 2
ROWS = 1024
HALF = 3 * B // 2
GR = HALF // CHIPS // 2
MM = ((1,), (0,))
TM = ((0,), (0,))
ROUTE = (
    0xBFDC2745, 0x0163E98A, 0xFCDB3245, 0x10769EA8, 0xEFD96704, 0x51328CBA, 0xEF897614, 0x0325CABD,
    0x26104573, 0xFDCB9AE8, 0x30175264, 0xCDEFAB98, 0x42310576, 0xC9EF8BAD, 0x30124765, 0x98FEABCD,
    0x52641073, 0xB89FAEDC, 0x27450631, 0x98EABFDC, 0x76501432, 0xCDBAFE89, 0x76410532, 0xDAB9FC8E,
    0x3457BCDA, 0x8EF90621, 0x4536DCBF, 0xEA982710, 0x6057FCDE, 0xAB892314, 0x45679EF8, 0xABDC2310,
)
Y_ORDER = (2, 1, 3)
Z_ORDER = (1, 3, 2)
SWAP = [(0, 1), (1, 0)]
VM = pl.BlockSpec(memory_space=pltpu.VMEM)
SM = pl.BlockSpec(memory_space=pltpu.SMEM)
HBM = pl.BlockSpec(memory_space=pltpu.HBM)
LONG = pl.CostEstimate(flops=20 << 30, bytes_accessed=8 << 20, transcendentals=0)
LONGER = pl.CostEstimate(flops=20 << 30, bytes_accessed=8 << 20, transcendentals=0)
PARAMS = pltpu.CompilerParams(vmem_limit_bytes=VMEM_LIMIT)


def split(value):
    high = value.astype(BF16)
    return high, (value - high.astype(F32)).astype(BF16)


def dot3(left, right, dims):
    lh, ll = left
    rh, rl = right
    go = functools.partial(lax.dot_general, dimension_numbers=(dims, ((), ())), preferred_element_type=F32)
    return go(lh, rh) + (go(lh, rl) + go(ll, rh))


def in_hbm(value):
    return pltpu.with_memory_space_constraint(value, pltpu.HBM)


def flag(listed, block):
    return jnp.max(jnp.where(listed == block, 1.0, 0.0), axis=1, keepdims=True)


def product_rows(s_ref, low, high, z):
    return dot3(split(s_ref[pl.ds(low, high - low)].reshape((high - low) * CH, ROWS)), z, MM)


def send_kernel(w_ref, s_hbm, two_hbm, one_hbm, top_hbm, b2_hbm, b1_hbm, p_ref, zh_ref, zl_ref, keep_ref, part_ref,
                s_ref, two_ref, one_ref, top_ref, b2_ref, b1_ref, sems):
    per = CHIPS // STEPS
    blocks = ROWS // B

    def rows_of(core, i):
        return s_hbm.at[pl.ds(i * per, per), pl.ds(pl.multiple_of(core * CH, CH), CH), :]

    pairs = [(b2_hbm, b2_ref), (b1_hbm, b1_ref), (top_hbm, top_ref)]
    for k in range(blocks):
        rows = pl.ds(k * B, B)
        pairs += [(two_hbm.at[rows], two_ref.at[rows]), (one_hbm.at[rows], one_ref.at[rows])]
    for i in range(STEPS):
        pairs.append((rows_of(1 - w_ref[1], i), s_ref.at[pl.ds(i * per, per)]))
    for i in range(STEPS):
        pairs.append((rows_of(w_ref[1], i), keep_ref.at[pl.ds(i * per, per)]))
    copies = [pltpu.make_async_copy(src, dst, sems.at[i]) for i, (src, dst) in enumerate(pairs)]
    for copy in copies:
        copy.start()
    for copy in copies[:3]:
        copy.wait()
    top = split(top_ref[...])
    first = w_ref[0] * blocks
    for k in range(blocks):
        copies[3 + 2 * k].wait()
        copies[4 + 2 * k].wait()
        rows = pl.ds(k * B, B)
        live_two = two_ref[rows, :] * flag(b2_ref[...], first + k)
        live_one = one_ref[rows, :] * flag(b1_ref[...], first + k)
        h2, l2 = split(live_two)
        hw, lw = split(live_one - dot3((h2, l2), top, MM))
        zh_ref[rows, :B] = h2
        zl_ref[rows, :B] = l2
        zh_ref[rows, B:] = hw
        zl_ref[rows, B:] = lw
    chunk = pl.ds(pl.multiple_of(w_ref[3] * CH, CH), CH)
    part_ref[:, :B] = two_ref[chunk, :]
    part_ref[:, B:] = one_ref[chunk, :]
    z = (zh_ref[...], zl_ref[...])
    for i in range(STEPS):
        copies[3 + 2 * blocks + i].wait()
        p_ref[pl.ds(i * per * CH, per * CH), :] = product_rows(s_ref, i * per, (i + 1) * per, z)
    for copy in copies[3 + 2 * blocks + STEPS:]:
        copy.wait()


def keep_kernel(s_ref, zh_ref, zl_ref, got_ref, p_ref):
    per = CHIPS // STEPS
    z = (zh_ref[...], zl_ref[...])
    for i in range(STEPS):
        rows = pl.ds(i * per * CH, per * CH)
        p_ref[rows, :] = got_ref[rows, :] + product_rows(s_ref, i * per, (i + 1) * per, z)


def products(where, sigma, two, one, top, b2, b1):
    sigma = sigma.reshape(CHIPS, 2 * CH, ROWS)
    shape_p = jax.ShapeDtypeStruct((CHIPS * CH, W), F32)
    shape_z = jax.ShapeDtypeStruct((ROWS, W), BF16)
    shape_s = jax.ShapeDtypeStruct((CHIPS, CH, ROWS), F32)
    send, zh, zl, mine, part = pl.pallas_call(
        send_kernel,
        in_specs=[SM] + [HBM] * 6,
        out_specs=[VM] * 5,
        out_shape=[shape_p, shape_z, shape_z, shape_s, jax.ShapeDtypeStruct((CH, W), F32)],
        scratch_shapes=[
            pltpu.VMEM(shape_s.shape, F32),
            pltpu.VMEM((ROWS, B), F32),
            pltpu.VMEM((ROWS, B), F32),
            pltpu.VMEM((B, B), F32),
            pltpu.VMEM(b2.shape, jnp.int32),
            pltpu.VMEM(b1.shape, jnp.int32),
            pltpu.SemaphoreType.DMA((3 + 2 * (ROWS // B) + 2 * STEPS,)),
        ],
        compiler_params=PARAMS,
        cost_estimate=LONG,
        name="product_send",
    )(where, *map(in_hbm, (sigma, two, one, top, b2, b1)))

    got = lax.ppermute(send, "c", SWAP)
    pair = pl.pallas_call(
        keep_kernel,
        in_specs=[VM] * 4,
        out_specs=VM,
        out_shape=shape_p,
        compiler_params=PARAMS,
        cost_estimate=LONG,
        name="product_keep",
    )(mine, zh, zl, got)
    return pair, part


def sum_kernel(parts, in_ref, after_ref, out_ref):
    rows = out_ref.shape[0]
    total = in_ref[pl.ds(0, rows), :]
    for k in range(1, parts):
        total = total + in_ref[pl.ds(k * rows, rows), :]
    out_ref[...] = total


def sum_parts(value, after):
    rows = value.shape[0] // CHIPS
    return pl.pallas_call(
        functools.partial(sum_kernel, CHIPS),
        in_specs=[VM, pl.BlockSpec(memory_space=pl.ANY)],
        out_specs=VM,
        out_shape=jax.ShapeDtypeStruct((rows, W), F32),
        compiler_params=PARAMS,
        name="sum_parts",
    )(value, after)


def ring_total(order, refs):
    by = dict(zip(order, refs[1:]))
    return (refs[0][...] + by[2][...]) + (by[1][...] + by[3][...])


def ring_kernel(order, *refs):
    refs[4][...] = ring_total(order, refs)


def chunk_kernel(w_ref, own_ref, b2_ref, b1_ref, top_ref, inv2_ref, inv1_ref, chunk_ref, it_ref, base_ref):
    block = w_ref[2]
    two = own_ref[:, :B] * -flag(b2_ref[...], block)
    one = own_ref[:, B:] * -flag(b1_ref[...], block)
    for q in range(CHIPS):
        chunk_ref[pl.ds(q * CH, CH), :B] = two
        chunk_ref[pl.ds(q * CH, CH), B:] = one
    top = split(top_ref[...])
    it = dot3(split(inv2_ref[...]), top, MM)
    it_ref[...] = it
    base_ref[...] = inv1_ref[...] + dot3(top, split(it), TM)


def spread_kernel(order, *refs):
    total = ring_total(order, refs)
    for q in range(CHIPS):
        refs[4][pl.ds(q * GR, GR), :] = total


def rows_kernel(w_ref, z_ref, top_ref, b2_ref, b1_ref, live_ref):
    block = w_ref[2]
    live_two = z_ref[:, :B] * flag(b2_ref[...], block)
    live_one = z_ref[:, B:] * flag(b1_ref[...], block)
    live_ref[:, :B] = live_two
    live_ref[:, B:] = live_one - dot3(split(live_two), split(top_ref[...]), MM)


def gram_kernel(w_ref, own_ref, oth_ref, z_own_ref, z_oth_ref, g_ref):
    def place(parts):
        rows = 0
        for part in parts:
            for low in range(0, part.shape[0], 8):
                q, rest = divmod(rows + low, 2 * GR)
                h, row = divmod(rest, GR)
                g_ref[pl.ds(q * GR + row, 8), pl.ds(h * B, B)] = part[low:low + 8]
            rows += part.shape[0]

    z = split(jnp.concatenate([z_own_ref[...], z_oth_ref[...]], axis=0))

    def columns(pair, low, high):
        return [v[:, low:high] for v in pair]

    @pl.when(w_ref[1] == 0)
    def _():
        y = split(jnp.concatenate([own_ref[...], oth_ref[...]], axis=0))
        place((
            dot3(columns(z, 0, B), columns(y, 0, B), TM),
            dot3(columns(z, 0, B // 2), columns(y, B, W), TM),
        ))

    @pl.when(w_ref[1] == 1)
    def _():
        y = split(jnp.concatenate([own_ref[:, B:], oth_ref[:, B:]], axis=0))
        place((dot3(columns(z, B // 2, B), y, TM), dot3(columns(z, B, W), y, TM)))


def assemble_kernel(w_ref, own_ref, oth_ref, c2_ref, c1_ref):
    mine = w_ref[1]
    for core, ref in ((mine, own_ref), (1 - mine, oth_ref)):
        for q in range(CHIPS):
            rows = pl.ds(pl.multiple_of(q * 2 * CH + core * CH, CH), CH)
            c2_ref[rows, :] = ref[pl.ds(q * CH, CH), :B]
            c1_ref[rows, :] = ref[pl.ds(q * CH, CH), B:]


def last_kernel(w_ref, own_ref, oth_ref, inv2_ref, it_ref, base_ref, d2_ref, cp_ref, d1_ref):
    def write(refs):
        for half, ref in enumerate(refs):
            for q in range(CHIPS):
                for h in range(2):
                    at = half * HALF + q * 2 * GR + h * GR
                    piece = ref[pl.ds(q * GR, GR), pl.ds(h * B, B)]
                    for low in range(0, GR, 8):
                        which, row = divmod(at + low, B)
                        rows = pl.ds(row, 8)
                        value = piece[low:low + 8]
                        if which == 0:
                            d2_ref[rows, :] = inv2_ref[rows, :] + value
                        elif which == 1:
                            cp_ref[rows, :] = value - it_ref[rows, :]
                        else:
                            d1_ref[rows, :] = base_ref[rows, :] + value

    @pl.when(w_ref[1] == 0)
    def _():
        write((own_ref, oth_ref))

    @pl.when(w_ref[1] == 1)
    def _():
        write((oth_ref, own_ref))


def route(i, j):
    return (ROUTE[2 * j + (i >> 3)] >> (4 * (i & 7))) & 15


def a2a(value, axes):
    return lax.all_to_all(value, axes, 0, 0, tiled=True)


def ring(value, axis, order):
    return [value] + [lax.ppermute(value, axis, [(i, (i + k) % 4) for i in range(4)]) for k in order]


def per_device(sigma, two, one, top, blocks_two, blocks_one, inv2, inv1):
    z_hi, y, z_lo, x, c = (lax.axis_index(a) for a in AXES)
    row = z_hi * 4 + y
    chip = z_lo * 4 + x
    b2 = blocks_two.reshape(1, -1)
    b1 = blocks_one.reshape(1, -1)

    turn = [(i * 16 + j, j * 16 + route(i, j)) for i in range(16) for j in range(16)]
    word = jnp.uint32(ROUTE[0])
    for k, other in enumerate(ROUTE):
        word = jnp.where((chip * 2 + c) * 2 + lax.shift_right_logical(row, 3) == k, jnp.uint32(other), word)
    chunk = (lax.shift_right_logical(word, (4 * (row & 7)).astype(jnp.uint32)) & 15).astype(jnp.int32)
    where = jnp.stack([chip * 2 + c, c, row * 4 + lax.shift_right_logical(chip, 1), chunk]).astype(jnp.int32)
    pair, part = products(where, sigma, two, one, top, b2, b1)
    z_own = lax.ppermute(part, AXES, turn)
    y_parts = a2a(pair, ("zl", "x"))
    z_own = pl.pallas_call(
        rows_kernel,
        in_specs=[SM] + [VM] * 4,
        out_specs=VM,
        out_shape=jax.ShapeDtypeStruct((CH, W), F32),
        compiler_params=PARAMS,
        cost_estimate=LONGER,
        name="panel_rows",
    )(where, z_own, top, b2, b1)
    z_oth = lax.ppermute(z_own, "c", SWAP)
    own = sum_parts(y_parts, z_own)
    oth = lax.ppermute(own, "c", SWAP)
    parts = jax.ShapeDtypeStruct((CHIPS * GR, W), F32)
    g = pl.pallas_call(
        gram_kernel,
        in_specs=[SM] + [VM] * 4,
        out_specs=VM,
        out_shape=parts,
        compiler_params=PARAMS,
        name="gram",
    )(where, own, oth, z_own, z_oth)
    g, y_own = lax.optimization_barrier((g, own))
    g = a2a(g, ("zl", "x"))
    square = jax.ShapeDtypeStruct((B, B), F32)
    chunks, it, base = pl.pallas_call(
        chunk_kernel,
        in_specs=[SM] + [VM] * 6,
        out_specs=[VM] * 3,
        out_shape=[jax.ShapeDtypeStruct((CHIPS * CH, W), F32), square, square],
        compiler_params=PARAMS,
        name="chunks",
    )(where, y_own, b2, b1, top, inv2, inv1)
    chunks = a2a(chunks, ("zl", "x"))

    g = sum_parts(g, base)
    g = pl.pallas_call(
        functools.partial(ring_kernel, Y_ORDER), in_specs=[VM] * 4, out_specs=VM, out_shape=jax.ShapeDtypeStruct((GR, W), F32),
        compiler_params=PARAMS, name="ring_sum",
    )(*ring(g, "y", Y_ORDER))
    g = ring(g, "zh", Z_ORDER)
    g = pl.pallas_call(
        functools.partial(spread_kernel, Z_ORDER), in_specs=[VM] * 4, out_specs=VM, out_shape=parts, compiler_params=PARAMS, name="spread"
    )(*g)
    g = a2a(g, ("zl", "x"))

    column = jax.ShapeDtypeStruct((ROWS, B), F32)
    column_two, column_one = pl.pallas_call(
        assemble_kernel,
        in_specs=[SM] + [VM] * 2,
        out_specs=[VM] * 2,
        out_shape=[column] * 2,
        compiler_params=PARAMS,
        name="assemble",
    )(where, chunks, lax.ppermute(chunks, "c", SWAP))
    g_oth = lax.ppermute(g, "c", SWAP)
    base, column_two, column_one = lax.optimization_barrier((base, column_two, column_one))
    d2, cp, d1 = pl.pallas_call(
        last_kernel,
        in_specs=[SM] + [VM] * 5,
        out_specs=[VM] * 3,
        out_shape=[square] * 3,
        compiler_params=PARAMS,
        name="last",
    )(where, g, g_oth, inv2, it, base)

    return column_two, d2, column_one, cp, d1


def solution(mesh):
    fine = Mesh(mesh.devices.reshape(SIZES), AXES)
    prow = ("zh", "y")
    pcol = ("zl", "x", "c")
    in_specs = (P(prow, pcol), P(pcol, None), P(pcol, None), P(), P(), P(), P(), P())
    out_specs = (P(prow, None), P(), P(prow, None), P(), P())
    return jax.shard_map(
        per_device, mesh=fine, in_specs=in_specs, out_specs=out_specs, check_vma=False
    )
```

```python
import functools

import jax
import jax.numpy as jnp
from jax import lax
from jax.experimental import pallas as pl
from jax.experimental.pallas import tpu as pltpu
from jax.sharding import Mesh, PartitionSpec as P

F32 = jnp.float32
BF16 = jnp.bfloat16
VMEM_LIMIT = 24 * 1024 * 1024
AXES = ("zh", "y", "zl", "x", "c")
SIZES = (4, 4, 2, 4, 2)
B = 256
W = 2 * B
CH = 64
CHIPS = 8
STEPS = 1
ROWS = 1024
HALF = 3 * B // 2
GR = HALF // CHIPS // 2
MM = ((1,), (0,))
TM = ((0,), (0,))
ROUTE = (
    0xBFDC2745, 0x0163E98A, 0xFCDB3245, 0x10769EA8, 0xEFD96704, 0x51328CBA, 0xEF897614, 0x0325CABD,
    0x26104573, 0xFDCB9AE8, 0x30175264, 0xCDEFAB98, 0x42310576, 0xC9EF8BAD, 0x30124765, 0x98FEABCD,
    0x52641073, 0xB89FAEDC, 0x27450631, 0x98EABFDC, 0x76501432, 0xCDBAFE89, 0x76410532, 0xDAB9FC8E,
    0x3457BCDA, 0x8EF90621, 0x4536DCBF, 0xEA982710, 0x6057FCDE, 0xAB892314, 0x45679EF8, 0xABDC2310,
)
Y_ORDER = (2, 1, 3)
Z_ORDER = (1, 3, 2)
SWAP = [(0, 1), (1, 0)]
VM = pl.BlockSpec(memory_space=pltpu.VMEM)
SM = pl.BlockSpec(memory_space=pltpu.SMEM)
HBM = pl.BlockSpec(memory_space=pltpu.HBM)
LONG = pl.CostEstimate(flops=20 << 30, bytes_accessed=8 << 20, transcendentals=0)
LONGER = pl.CostEstimate(flops=20 << 30, bytes_accessed=8 << 20, transcendentals=0)
PARAMS = pltpu.CompilerParams(vmem_limit_bytes=VMEM_LIMIT)


def split(value):
    high = value.astype(BF16)
    return high, (value - high.astype(F32)).astype(BF16)


def dot3(left, right, dims):
    lh, ll = left
    rh, rl = right
    go = functools.partial(lax.dot_general, dimension_numbers=(dims, ((), ())), preferred_element_type=F32)
    return go(lh, rh) + (go(lh, rl) + go(ll, rh))


def in_hbm(value):
    return pltpu.with_memory_space_constraint(value, pltpu.HBM)


def flag(listed, block):
    return jnp.max(jnp.where(listed == block, 1.0, 0.0), axis=1, keepdims=True)


def product_rows(s_ref, low, high, z):
    return dot3(split(s_ref[pl.ds(low, high - low)].reshape((high - low) * CH, ROWS)), z, MM)


def send_kernel(w_ref, s_hbm, two_hbm, one_hbm, top_hbm, b2_hbm, b1_hbm, p_ref, zh_ref, zl_ref, keep_ref, part_ref,
                s_ref, two_ref, one_ref, top_ref, b2_ref, b1_ref, sems):
    per = CHIPS // STEPS
    blocks = ROWS // B

    def rows_of(core, i):
        return s_hbm.at[pl.ds(i * per, per), pl.ds(pl.multiple_of(core * CH, CH), CH), :]

    pairs = [(b2_hbm, b2_ref), (b1_hbm, b1_ref), (top_hbm, top_ref)]
    for k in range(blocks):
        rows = pl.ds(k * B, B)
        pairs += [(two_hbm.at[rows], two_ref.at[rows]), (one_hbm.at[rows], one_ref.at[rows])]
    for i in range(STEPS):
        pairs.append((rows_of(1 - w_ref[1], i), s_ref.at[pl.ds(i * per, per)]))
    for i in range(STEPS):
        pairs.append((rows_of(w_ref[1], i), keep_ref.at[pl.ds(i * per, per)]))
    copies = [pltpu.make_async_copy(src, dst, sems.at[i]) for i, (src, dst) in enumerate(pairs)]
    for copy in copies:
        copy.start()
    for copy in copies[:3]:
        copy.wait()
    top = split(top_ref[...])
    first = w_ref[0] * blocks
    for k in range(blocks):
        copies[3 + 2 * k].wait()
        copies[4 + 2 * k].wait()
        rows = pl.ds(k * B, B)
        live_two = two_ref[rows, :] * flag(b2_ref[...], first + k)
        live_one = one_ref[rows, :] * flag(b1_ref[...], first + k)
        h2, l2 = split(live_two)
        hw, lw = split(live_one - dot3((h2, l2), top, MM))
        zh_ref[rows, :B] = h2
        zl_ref[rows, :B] = l2
        zh_ref[rows, B:] = hw
        zl_ref[rows, B:] = lw
    chunk = pl.ds(pl.multiple_of(w_ref[3] * CH, CH), CH)
    part_ref[:, :B] = two_ref[chunk, :]
    part_ref[:, B:] = one_ref[chunk, :]
    z = (zh_ref[...], zl_ref[...])
    for i in range(STEPS):
        copies[3 + 2 * blocks + i].wait()
        p_ref[pl.ds(i * per * CH, per * CH), :] = product_rows(s_ref, i * per, (i + 1) * per, z)
    for copy in copies[3 + 2 * blocks + STEPS:]:
        copy.wait()


def keep_kernel(s_ref, zh_ref, zl_ref, got_ref, p_hbm, p_ref, sems):
    per = CHIPS // 2
    z = (zh_ref[...], zl_ref[...])
    copies = []
    for i in range(2):
        rows = pl.ds(i * per * CH, per * CH)
        p_ref[rows, :] = got_ref[rows, :] + product_rows(s_ref, i * per, (i + 1) * per, z)
        copies.append(pltpu.make_async_copy(p_ref.at[rows], p_hbm.at[rows], sems.at[i]))
        copies[i].start()
    for copy in copies:
        copy.wait()


def products(where, sigma, two, one, top, b2, b1):
    sigma = sigma.reshape(CHIPS, 2 * CH, ROWS)
    shape_p = jax.ShapeDtypeStruct((CHIPS * CH, W), F32)
    shape_z = jax.ShapeDtypeStruct((ROWS, W), BF16)
    shape_s = jax.ShapeDtypeStruct((CHIPS, CH, ROWS), F32)
    send, zh, zl, mine, part = pl.pallas_call(
        send_kernel,
        in_specs=[SM] + [HBM] * 6,
        out_specs=[VM] * 5,
        out_shape=[shape_p, shape_z, shape_z, shape_s, jax.ShapeDtypeStruct((CH, W), F32)],
        scratch_shapes=[
            pltpu.VMEM(shape_s.shape, F32),
            pltpu.VMEM((ROWS, B), F32),
            pltpu.VMEM((ROWS, B), F32),
            pltpu.VMEM((B, B), F32),
            pltpu.VMEM(b2.shape, jnp.int32),
            pltpu.VMEM(b1.shape, jnp.int32),
            pltpu.SemaphoreType.DMA((3 + 2 * (ROWS // B) + 2 * STEPS,)),
        ],
        compiler_params=PARAMS,
        cost_estimate=LONG,
        name="product_send",
    )(where, *map(in_hbm, (sigma, two, one, top, b2, b1)))

    got = lax.ppermute(send, "c", SWAP)
    pair = pl.pallas_call(
        keep_kernel,
        in_specs=[VM] * 4,
        out_specs=HBM,
        out_shape=shape_p,
        scratch_shapes=[pltpu.VMEM(shape_p.shape, F32), pltpu.SemaphoreType.DMA((2,))],
        compiler_params=PARAMS,
        cost_estimate=LONG,
        name="product_keep",
    )(mine, zh, zl, got)
    return pair, part


def sum_kernel(parts, in_ref, after_ref, out_ref):
    rows = out_ref.shape[0]
    total = in_ref[pl.ds(0, rows), :]
    for k in range(1, parts):
        total = total + in_ref[pl.ds(k * rows, rows), :]
    out_ref[...] = total


def sum_parts(value, after):
    rows = value.shape[0] // CHIPS
    return pl.pallas_call(
        functools.partial(sum_kernel, CHIPS),
        in_specs=[VM, pl.BlockSpec(memory_space=pl.ANY)],
        out_specs=VM,
        out_shape=jax.ShapeDtypeStruct((rows, W), F32),
        compiler_params=PARAMS,
        name="sum_parts",
    )(value, after)


def ring_total(order, refs):
    by = dict(zip(order, refs[1:]))
    return (refs[0][...] + by[2][...]) + (by[1][...] + by[3][...])


def ring_kernel(order, *refs):
    refs[4][...] = ring_total(order, refs)


def chunk_kernel(w_ref, own_ref, b2_ref, b1_ref, top_ref, inv2_ref, inv1_ref, chunk_ref, it_ref, base_ref):
    block = w_ref[2]
    two = own_ref[:, :B] * -flag(b2_ref[...], block)
    one = own_ref[:, B:] * -flag(b1_ref[...], block)
    for q in range(CHIPS):
        chunk_ref[pl.ds(q * CH, CH), :B] = two
        chunk_ref[pl.ds(q * CH, CH), B:] = one
    top = split(top_ref[...])
    it = dot3(split(inv2_ref[...]), top, MM)
    it_ref[...] = it
    base_ref[...] = inv1_ref[...] + dot3(top, split(it), TM)


def spread_kernel(order, *refs):
    total = ring_total(order, refs)
    for q in range(CHIPS):
        refs[4][pl.ds(q * GR, GR), :] = total


def rows_kernel(w_ref, z_ref, top_ref, b2_ref, b1_ref, live_ref):
    block = w_ref[2]
    live_two = z_ref[:, :B] * flag(b2_ref[...], block)
    live_one = z_ref[:, B:] * flag(b1_ref[...], block)
    live_ref[:, :B] = live_two
    live_ref[:, B:] = live_one - dot3(split(live_two), split(top_ref[...]), MM)


def gram_kernel(w_ref, own_ref, oth_ref, z_own_ref, z_oth_ref, g_ref):
    def place(parts):
        rows = 0
        for part in parts:
            for low in range(0, part.shape[0], 8):
                q, rest = divmod(rows + low, 2 * GR)
                h, row = divmod(rest, GR)
                g_ref[pl.ds(q * GR + row, 8), pl.ds(h * B, B)] = part[low:low + 8]
            rows += part.shape[0]

    z = split(jnp.concatenate([z_own_ref[...], z_oth_ref[...]], axis=0))

    def columns(pair, low, high):
        return [v[:, low:high] for v in pair]

    @pl.when(w_ref[1] == 0)
    def _():
        y = split(jnp.concatenate([own_ref[...], oth_ref[...]], axis=0))
        place((
            dot3(columns(z, 0, B), columns(y, 0, B), TM),
            dot3(columns(z, 0, B // 2), columns(y, B, W), TM),
        ))

    @pl.when(w_ref[1] == 1)
    def _():
        y = split(jnp.concatenate([own_ref[:, B:], oth_ref[:, B:]], axis=0))
        place((dot3(columns(z, B // 2, B), y, TM), dot3(columns(z, B, W), y, TM)))


def assemble_kernel(w_ref, own_ref, oth_ref, c2_ref, c1_ref):
    mine = w_ref[1]
    for core, ref in ((mine, own_ref), (1 - mine, oth_ref)):
        for q in range(CHIPS):
            rows = pl.ds(pl.multiple_of(q * 2 * CH + core * CH, CH), CH)
            c2_ref[rows, :] = ref[pl.ds(q * CH, CH), :B]
            c1_ref[rows, :] = ref[pl.ds(q * CH, CH), B:]


def last_kernel(w_ref, own_ref, oth_ref, inv2_ref, it_ref, base_ref, d2_ref, cp_ref, d1_ref):
    def write(refs):
        for half, ref in enumerate(refs):
            for q in range(CHIPS):
                for h in range(2):
                    at = half * HALF + q * 2 * GR + h * GR
                    piece = ref[pl.ds(q * GR, GR), pl.ds(h * B, B)]
                    for low in range(0, GR, 8):
                        which, row = divmod(at + low, B)
                        rows = pl.ds(row, 8)
                        value = piece[low:low + 8]
                        if which == 0:
                            d2_ref[rows, :] = inv2_ref[rows, :] + value
                        elif which == 1:
                            cp_ref[rows, :] = value - it_ref[rows, :]
                        else:
                            d1_ref[rows, :] = base_ref[rows, :] + value

    @pl.when(w_ref[1] == 0)
    def _():
        write((own_ref, oth_ref))

    @pl.when(w_ref[1] == 1)
    def _():
        write((oth_ref, own_ref))


def route(i, j):
    return (ROUTE[2 * j + (i >> 3)] >> (4 * (i & 7))) & 15


def a2a(value, axes):
    return lax.all_to_all(value, axes, 0, 0, tiled=True)


def ring(value, axis, order):
    return [value] + [lax.ppermute(value, axis, [(i, (i + k) % 4) for i in range(4)]) for k in order]


def per_device(sigma, two, one, top, blocks_two, blocks_one, inv2, inv1):
    z_hi, y, z_lo, x, c = (lax.axis_index(a) for a in AXES)
    row = z_hi * 4 + y
    chip = z_lo * 4 + x
    b2 = blocks_two.reshape(1, -1)
    b1 = blocks_one.reshape(1, -1)

    turn = [(i * 16 + j, j * 16 + route(i, j)) for i in range(16) for j in range(16)]
    word = jnp.uint32(ROUTE[0])
    for k, other in enumerate(ROUTE):
        word = jnp.where((chip * 2 + c) * 2 + lax.shift_right_logical(row, 3) == k, jnp.uint32(other), word)
    chunk = (lax.shift_right_logical(word, (4 * (row & 7)).astype(jnp.uint32)) & 15).astype(jnp.int32)
    where = jnp.stack([chip * 2 + c, c, row * 4 + lax.shift_right_logical(chip, 1), chunk]).astype(jnp.int32)
    pair, part = products(where, sigma, two, one, top, b2, b1)
    z_own = lax.ppermute(part, AXES, turn)
    y_parts = a2a(pair, ("zl", "x"))
    z_own = pl.pallas_call(
        rows_kernel,
        in_specs=[SM] + [VM] * 4,
        out_specs=VM,
        out_shape=jax.ShapeDtypeStruct((CH, W), F32),
        compiler_params=PARAMS,
        cost_estimate=LONGER,
        name="panel_rows",
    )(where, z_own, top, b2, b1)
    z_oth = lax.ppermute(z_own, "c", SWAP)
    own = sum_parts(y_parts, z_own)
    oth = lax.ppermute(own, "c", SWAP)
    parts = jax.ShapeDtypeStruct((CHIPS * GR, W), F32)
    g = pl.pallas_call(
        gram_kernel,
        in_specs=[SM] + [VM] * 4,
        out_specs=VM,
        out_shape=parts,
        compiler_params=PARAMS,
        name="gram",
    )(where, own, oth, z_own, z_oth)
    g, y_own = lax.optimization_barrier((g, own))
    g = a2a(g, ("zl", "x"))
    square = jax.ShapeDtypeStruct((B, B), F32)
    chunks, it, base = pl.pallas_call(
        chunk_kernel,
        in_specs=[SM] + [VM] * 6,
        out_specs=[VM] * 3,
        out_shape=[jax.ShapeDtypeStruct((CHIPS * CH, W), F32), square, square],
        compiler_params=PARAMS,
        name="chunks",
    )(where, y_own, b2, b1, top, inv2, inv1)
    chunks = a2a(chunks, ("zl", "x"))

    g = sum_parts(g, base)
    g = pl.pallas_call(
        functools.partial(ring_kernel, Y_ORDER), in_specs=[VM] * 4, out_specs=VM, out_shape=jax.ShapeDtypeStruct((GR, W), F32),
        compiler_params=PARAMS, name="ring_sum",
    )(*ring(g, "y", Y_ORDER))
    g = ring(g, "zh", Z_ORDER)
    g = pl.pallas_call(
        functools.partial(spread_kernel, Z_ORDER), in_specs=[VM] * 4, out_specs=VM, out_shape=parts, compiler_params=PARAMS, name="spread"
    )(*g)
    g = a2a(g, ("zl", "x"))

    column = jax.ShapeDtypeStruct((ROWS, B), F32)
    column_two, column_one = pl.pallas_call(
        assemble_kernel,
        in_specs=[SM] + [VM] * 2,
        out_specs=[VM] * 2,
        out_shape=[column] * 2,
        compiler_params=PARAMS,
        name="assemble",
    )(where, chunks, lax.ppermute(chunks, "c", SWAP))
    g_oth = lax.ppermute(g, "c", SWAP)
    base, column_two, column_one = lax.optimization_barrier((base, column_two, column_one))
    d2, cp, d1 = pl.pallas_call(
        last_kernel,
        in_specs=[SM] + [VM] * 5,
        out_specs=[VM] * 3,
        out_shape=[square] * 3,
        compiler_params=PARAMS,
        name="last",
    )(where, g, g_oth, inv2, it, base)

    return column_two, d2, column_one, cp, d1


def solution(mesh):
    fine = Mesh(mesh.devices.reshape(SIZES), AXES)
    prow = ("zh", "y")
    pcol = ("zl", "x", "c")
    in_specs = (P(prow, pcol), P(pcol, None), P(pcol, None), P(), P(), P(), P(), P())
    out_specs = (P(prow, None), P(), P(prow, None), P(), P())
    return jax.shard_map(
        per_device, mesh=fine, in_specs=in_specs, out_specs=out_specs, check_vma=False
    )
```
